256 devices in a mesh: ep: 64 (over x, z, core), edp: 4 (over y).
Axes of the slice: x: 4, y: 4, z: 8, core: 2. Of those that a mesh axis runs over, the one named last changes fastest.
Arguments:
- inputs: bfloat16 [32768, 3584], P(('ep', 'edp')), may hold values from -6 to 6
- out_grad: bfloat16 [32768, 3584], P(('ep', 'edp')), may hold values from -6 to 6
- expert_ids: int32 [32768, 2], P(('ep', 'edp')), may hold values from 0 to 63, all different within a row; in each aligned block of 128 rows (0 to 127, 128 to 255, ...) at most 6 rows name the same one
- route_weight: float32 [32768, 2], P(('ep', 'edp')), may hold values from 0.05 to 0.8
- gate_up_weight: bfloat16 [64, 2, 3584, 1024], P('ep', None, None, 'edp'), may hold values from -0.09375 to 0.09375
- down_weight: bfloat16 [64, 1024, 3584], P('ep', 'edp'), may hold values from -0.1875 to 0.1875
- down_moment: bfloat16 [64, 1024, 3584], P('ep', 'edp'), may hold values from -8 to 8
- down_second: bfloat16 [64, 1024, 3584], P('ep', 'edp'), may hold values from 0.5 to 50
Outputs:
- input_grad: bfloat16 [32768, 3584], P(('ep', 'edp'))
- new_down: bfloat16 [64, 1024, 3584], P('ep', 'edp')
The draws below stay inside these ranges and needn't reach their ends.
Inputs may be any that keep to these rules, and one draw needn't show every extreme that they name: `expert_ids`: A token names 2 different experts. Among the rows of one device no expert is named more than 6 times, a bound that some block reaches.
All inputs are finite; a program needn't handle non-finite values.
Results may differ from the reference program's by a relative error of at most 0.0065.
Values may be sent and summed in bfloat16 or wider, within the bound.
No kernel may reach another device: no remote copies, remote signals or barrier semaphores. Data moves between devices by JAX's collectives and lax.ppermute only.
A program may use at most 128 MiB of HBM per device.

```python
import math
import jax
import jax.numpy as jnp
import numpy as np
from jax import lax

D = 3584
H = 1024
TOP = 2
TOK_DEV = 128
EXPERTS = 64
CAP = 6
TOKENS = 32768


def block_levels(own_key, extent, cuts, smallest, high):
    loudness, own = 1.0, jax.random.fold_in(own_key, 6)
    for dim, blocks in cuts:
        steps = jnp.exp(jax.random.uniform(jax.random.fold_in(own, dim), (blocks,), jnp.float32, smallest / len(cuts), high / len(cuts)))
        loudness = loudness * jnp.repeat(steps, extent[dim] // blocks).reshape([-1 if axis == dim else 1 for axis in range(len(extent))])
    return loudness


def assign_block(own_key, own, number, rows, count, top, most, lean):
    ranking = jax.random.permutation(own_key, count)
    heavy_load, usual = portions_of(count, rows * top, most, lean, True), portions_of(count, rows * top, most, lean, False)
    places = jnp.arange(count)

    def named(lengths, turn):
        used = int((lengths > 0).sum())
        fixed = max(1, used // 4)
        shifted = fixed + (places - fixed + turn * (used - fixed)) % max(1, count - fixed)
        return jnp.zeros((count,), jnp.int32).at[ranking[jnp.where(places < fixed, places, shifted)]].set(jnp.asarray(lengths, jnp.int32))

    lengths = jnp.where(number % 4 == 0, named(heavy_load, number // 4), named(usual, number - number // 4 - 1))
    mixed = jax.random.permutation(jax.random.fold_in(own, 3), count)
    source_of, taker = mixed[0:count // 2 * 2:2], mixed[1:count // 2 * 2:2]
    slack = jnp.minimum(lengths[source_of] - 1, most - lengths[taker]) // 2
    slack = jnp.where((source_of == ranking[0]) | (taker == ranking[0]) | (lengths[taker] == 0), 0, jnp.maximum(slack, 0))
    shifted = jax.random.randint(jax.random.fold_in(own, 4), (count // 2,), 0, 1 << 20) % (slack + 1)
    lengths = lengths.at[source_of].add(-shifted).at[taker].add(shifted)
    items = jnp.searchsorted(jnp.cumsum(lengths), jnp.arange(rows * top), side="right").astype(jnp.int32)
    listing = items.reshape(top, rows).T
    listing = listing[jax.random.permutation(jax.random.fold_in(own, 1), rows)]
    turn = jax.random.randint(jax.random.fold_in(own, 2), (rows, 1), 0, top)
    return jnp.take_along_axis(listing, (jnp.arange(top)[None, :] + turn) % top, axis=1)


def portions_of(number_of, total, bound, skew, full):
    portions = [(1 << 20) // math.isqrt(standing ** skew) + 1 for standing in range(1, number_of + 1)]
    largest = bound if full else min(bound, max(-(-total // number_of), total * portions[0] // sum(portions)))
    least = 1 if total - largest >= number_of - 1 else 0
    holding, surplus = [largest] + [least] * (number_of - 1), total - largest - least * (number_of - 1)
    while surplus > 0:
        candidates = [i for i in range(1, number_of) if holding[i] < largest] or [i for i in range(1, number_of) if holding[i] < bound]
        whole, budget = sum([portions[i] for i in candidates]), surplus
        for i in candidates:
            addition = min(bound - holding[i], max(1, budget * portions[i] // whole), surplus)
            holding[i] = holding[i] + addition
            surplus = surplus - addition
    return np.array(holding)


def bell_draw(key, extent, deviation, bound, cuts=(), held_as=jnp.bfloat16):
    entries = jax.random.normal(key, extent, jnp.float32) * deviation
    if len(cuts) > 0:
        entries = block_levels(key, extent, cuts, -0.22, 0.18) * entries
    return jnp.clip(entries, min=-bound, max=bound).astype(held_as)


def setup_inputs(seed: int = 0) -> dict:
    key_list = jax.random.split(jax.random.key(seed), 9)
    inputs = bell_draw(key_list[0], (TOKENS, D), 1.0, 6.0, ((0, 256),))
    out_grad = bell_draw(key_list[1], (TOKENS, D), 1.0, 6.0, ((0, 256),))
    expert_ids_keys = jax.random.split(jax.random.fold_in(key_list[2], 1), TOKENS // TOK_DEV)
    expert_ids_turns = jax.random.permutation(jax.random.fold_in(key_list[2], 3), TOKENS // TOK_DEV)
    expert_ids = jax.vmap(lambda own, number: assign_block(jax.random.fold_in(key_list[2], 2), own, number, TOK_DEV, EXPERTS, TOP, CAP, 2))(expert_ids_keys, expert_ids_turns).reshape((TOKENS, TOP))
    route_weight = jnp.clip(jnp.exp(math.log(0.8) - 2.7725887 * jax.random.uniform(key_list[3], (TOKENS, TOP), jnp.float32) ** block_levels(key_list[3], (TOKENS, TOP), ((0, 256),), -0.2, 0.2)), 0.05, 0.8)
    gate_up_weight = bell_draw(key_list[4], (EXPERTS, 2, D, H), D ** -0.5, 0.09375, ((0, 64), (3, 4)))
    down_weight = bell_draw(key_list[5], (EXPERTS, H, D), H ** -0.5, 0.1875, ((0, 64), (1, 4)))
    down_moment = bell_draw(key_list[6], (EXPERTS, H, D), 2.0, 8.0, ((0, 64), (1, 4)))
    down_second = jnp.clip(jnp.exp(math.log(50.0) - 4.6051702 * jax.random.uniform(key_list[7], (EXPERTS, H, D), jnp.float32) ** block_levels(key_list[7], (EXPERTS, H, D), ((0, 64), (1, 4)), -0.2, 0.2)), 0.5, 50.0).astype(jnp.bfloat16)
    return {"inputs": inputs, "out_grad": out_grad, "expert_ids": expert_ids, "route_weight": route_weight, "gate_up_weight": gate_up_weight, "down_weight": down_weight, "down_moment": down_moment, "down_second": down_second}


def slot_table(ids_block, experts, capacity):
    flat = ids_block.reshape(-1).astype(jnp.int32)
    onehot = (flat[:, None] == jnp.arange(experts, dtype=jnp.int32)[None, :]).astype(jnp.int32)
    rank = lax.optimization_barrier(jnp.sum((jnp.cumsum(onehot, axis=0) - onehot) * onehot, axis=1)).astype(jnp.int32)
    dest = (flat * capacity + rank).astype(jnp.int32)
    count = flat.shape[0]
    table = jnp.full((experts * capacity,), count, jnp.int32).at[dest].set(jnp.arange(count, dtype=jnp.int32))
    return table

def derivs(gate, upper, dh):
    sig = jax.nn.sigmoid(gate)
    dgate = (dh * upper * sig * (1.0 + gate * (1.0 - sig))).astype(jnp.bfloat16)
    dup = (dh * gate * sig).astype(jnp.bfloat16)
    return (dgate, dup)

def adamw(param, moment, second, grad):
    first = 0.9 * moment.astype(jnp.float32) + 0.1 * grad
    other = 0.95 * second.astype(jnp.float32) + 0.05 * grad * grad
    first_hat = first / (1.0 - 0.9 ** 10)
    other_hat = other / (1.0 - 0.95 ** 10)
    weight = param.astype(jnp.float32)
    return (weight - 0.01 * (first_hat / (jnp.sqrt(other_hat) + 1e-08) + 0.1 * weight)).astype(jnp.bfloat16)

def reference(inputs, out_grad, expert_ids, route_weight, gate_up_weight, down_weight, down_moment, down_second):
    blocks = TOKENS // TOK_DEV
    per = TOK_DEV * TOP
    tables = jax.vmap(lambda block: slot_table(block, EXPERTS, CAP))(expert_ids.reshape(blocks, per))
    live = tables < per
    offsets = (jnp.arange(blocks, dtype=jnp.int32) * per)[:, None]
    glob = jnp.where(live, tables + offsets, 0).astype(jnp.int32)
    glob = glob.reshape(blocks, EXPERTS, CAP).transpose(1, 0, 2).reshape(EXPERTS, blocks * CAP)
    live = live.reshape(blocks, EXPERTS, CAP).transpose(1, 0, 2).reshape(EXPERTS, blocks * CAP)
    flat_weight = route_weight.reshape(-1)

    def one_expert(total, item):
        index, alive, gate_up, down, moment, second = item
        tokens_of = (index // TOP).astype(jnp.int32)
        rows_in = jnp.where(alive[:, None], inputs[tokens_of], 0).astype(jnp.bfloat16)
        weights_of = jnp.where(alive, flat_weight[index], 0.0)
        scaled = (weights_of[:, None] * out_grad[tokens_of].astype(jnp.float32)).astype(jnp.bfloat16)
        gate = jnp.dot(rows_in, gate_up[0], preferred_element_type=jnp.float32)
        upper = jnp.dot(rows_in, gate_up[1], preferred_element_type=jnp.float32)
        sig = jax.nn.sigmoid(gate)
        hidden = (gate * sig * upper).astype(jnp.bfloat16)
        dh = lax.dot_general(scaled, down, (((1,), (1,)), ((), ())), preferred_element_type=jnp.float32)
        dgate, dup = derivs(gate, upper, dh)
        part = lax.dot_general(dgate, gate_up[0], (((1,), (1,)), ((), ())), preferred_element_type=jnp.float32)
        part = part + lax.dot_general(dup, gate_up[1], (((1,), (1,)), ((), ())), preferred_element_type=jnp.float32)
        part = part.astype(jnp.bfloat16)
        grad = lax.dot_general(hidden, scaled, (((0,), (0,)), ((), ())), preferred_element_type=jnp.float32)
        total = total.at[tokens_of].add(jnp.where(alive[:, None], part.astype(jnp.float32), 0.0))
        return (total, adamw(down, moment, second, grad))
    start = jnp.zeros((TOKENS, D), jnp.float32)
    total, new_down = lax.scan(one_expert, start, (glob, live, gate_up_weight, down_weight, down_moment, down_second))
    return (total.astype(jnp.bfloat16), new_down)
```

```python
import jax
import jax.numpy as jnp
from jax import lax
from jax.experimental import pallas as pl
from jax.experimental.pallas import tpu as pltpu
from jax.sharding import PartitionSpec as P

BF = jnp.bfloat16
F32 = jnp.float32


def cut_of(width):
    return 4 if width % 512 == 0 else 1


def as_column(row):
    n = row.shape[1]
    eye = lax.broadcasted_iota(jnp.int32, (n, n), 0) == lax.broadcasted_iota(jnp.int32, (n, n), 1)
    return jnp.sum(jnp.where(eye, jnp.broadcast_to(row, (n, n)), 0), axis=1, keepdims=True)


def slots_kernel(capacity, ids_ref, dest_ref):
    top, n = ids_ref.shape
    earlier = lax.broadcasted_iota(jnp.int32, (n, n), 0) < lax.broadcasted_iota(jnp.int32, (n, n), 1)
    columns = [as_column(ids_ref[k : k + 1, :]) for k in range(top)]
    for k in range(top):
        row = ids_ref[k : k + 1, :]
        rank = jnp.zeros((1, n), jnp.int32)
        for j in range(top):
            same = (jnp.broadcast_to(columns[j], (n, n)) == jnp.broadcast_to(row, (n, n))) & earlier
            rank = rank + jnp.sum(same.astype(jnp.int32), axis=0, keepdims=True)
            if j < k:
                rank = rank + (ids_ref[j : j + 1, :] == row).astype(jnp.int32)
        dest_ref[k : k + 1, :] = row * capacity + rank


def make_dispatch(weighted, cut, rows_total, width, block):
    piece = width // cut

    def kernel(dest_ref, weight_ref, rows_ref, out_ref):
        top, n = dest_ref.shape
        base = pl.program_id(0) * block
        index = lax.broadcasted_iota(jnp.int32, (block, cut * n), 0) + base
        part = lax.broadcasted_iota(jnp.int32, (1, cut * n), 1) // n
        hits = []
        for k in range(top):
            key = jnp.concatenate([dest_ref[k : k + 1, :]] * cut, axis=1) * cut + part
            hits.append(index == jnp.broadcast_to(key, index.shape))
        onehot = hits[0]
        for hit in hits[1:]:
            onehot = onehot | hit
        stacked = jnp.concatenate(
            [rows_ref[:, q * piece : (q + 1) * piece] for q in range(cut)], axis=0
        )
        picked = jnp.dot(
            onehot.astype(F32).astype(BF), stacked, preferred_element_type=F32
        )
        if weighted:
            scale = jnp.zeros((block, 1), F32)
            for k in range(top):
                w = jnp.concatenate([weight_ref[k : k + 1, :]] * cut, axis=1)
                scale = scale + jnp.sum(
                    jnp.where(hits[k], jnp.broadcast_to(w, index.shape), 0.0), axis=1, keepdims=True
                )
            picked = picked * scale
        out_ref[...] = picked.astype(BF)

    def call(dest, weight, rows):
        top, n = dest.shape
        return pl.pallas_call(
            kernel,
            grid=(rows_total // block,),
            in_specs=[
                pl.BlockSpec((top, n), lambda i: (0, 0)),
                pl.BlockSpec((top, n), lambda i: (0, 0)),
                pl.BlockSpec((n, width), lambda i: (0, 0)),
            ],
            out_specs=pl.BlockSpec((block, piece), lambda i: (i, 0)),
            out_shape=jax.ShapeDtypeStruct((rows_total, piece), BF),
            compiler_params=pltpu.CompilerParams(vmem_limit_bytes=40 << 20),
            name="dispatch_weighted" if weighted else "dispatch",
            cost_estimate=pl.CostEstimate(
                flops=(20 if weighted else 2) * rows_total * cut * n * piece, bytes_accessed=4 * rows_total * piece, transcendentals=0
            ),
        )(dest, weight, rows)

    return call


def combine(dest, back, width):
    rows_total, piece = back.shape
    cut = width // piece
    top, n = dest.shape

    def kernel(dest_ref, back_ref, out_ref):
        columns = [as_column(dest_ref[k : k + 1, :]) for k in range(top)]
        lane = lax.broadcasted_iota(jnp.int32, (n, rows_total), 1)
        for q in range(cut):
            hit = lane == jnp.broadcast_to(columns[0] * cut + q, lane.shape)
            for k in range(1, top):
                hit = hit | (lane == jnp.broadcast_to(columns[k] * cut + q, lane.shape))
            out_ref[:, q * piece : (q + 1) * piece] = jnp.dot(
                hit.astype(F32).astype(BF), back_ref[...], preferred_element_type=F32
            ).astype(BF)

    return pl.pallas_call(
        kernel,
        out_shape=jax.ShapeDtypeStruct((n, width), BF),
        compiler_params=pltpu.CompilerParams(vmem_limit_bytes=40 << 20),
        name="combine",
        cost_estimate=pl.CostEstimate(
            flops=2 * n * rows_total * width, bytes_accessed=2 * rows_total * piece, transcendentals=0
        ),
    )(dest, back)


def adamw(param, moment, second, grad):
    first = 0.9 * moment.astype(F32) + 0.1 * grad
    other = 0.95 * second.astype(F32) + 0.05 * grad * grad
    first_hat = first / (1.0 - 0.9**10)
    other_hat = other / (1.0 - 0.95**10)
    weight = param.astype(F32)
    return (weight - 0.01 * (first_hat / (jnp.sqrt(other_hat) + 1e-08) + 0.1 * weight)).astype(BF)


def dot_t(left, right):
    return lax.dot_general(left, right, (((1,), (1,)), ((), ())), preferred_element_type=F32)


def t_dot(left, right):
    return lax.dot_general(left, right, (((0,), (0,)), ((), ())), preferred_element_type=F32)


def tie(value, *others):
    return lax.optimization_barrier((value,) + others)[0]


def back_kernel(count, first, last, s_ref, *refs):
    gates, uppers = refs[:count], refs[count : 2 * count]
    refs = refs[2 * count :]
    if not first:
        base_ref, refs = refs[0], refs[1:]
    downs, ups = refs[: 2 * count], refs[2 * count : 4 * count]
    out_ref, down_buf, up_buf, grad_buf = refs[4 * count : 4 * count + 4]
    spread, sems = refs[4 * count + 4 :] if last else (None, refs[-1])
    rows = s_ref.shape[0]
    half = down_buf.shape[1] // 2
    unit = 2 * half
    piece = up_buf.shape[0] // 4
    down_copies, up_copies = [], []
    for i, (ref, index) in enumerate(downs):
        source = ref if index is None else ref.at[pl.ds(index * half, half), :]
        down_copies.append(
            pltpu.make_async_copy(
                source, down_buf.at[i // 2, pl.ds((i % 2) * half, half), :], sems.at[i]
            )
        )
    for i, (ref, index) in enumerate(ups):
        source = ref if index is None else ref.at[index]
        up_copies.append(
            pltpu.make_async_copy(source, up_buf.at[:, pl.ds(i * unit, unit)], sems.at[2 * count + i])
        )
    for copy in down_copies + up_copies:
        copy.start()
    for q in range(count):
        down_copies[2 * q].wait()
        down_copies[2 * q + 1].wait()
        dh = dot_t(s_ref[...], down_buf[q])
        gate, upper = gates[q][...], uppers[q][...]
        sig = jax.nn.sigmoid(gate)
        grad_buf[:, (2 * q) * unit : (2 * q + 1) * unit] = (
            dh * upper * sig * (1.0 + gate * (1.0 - sig))
        ).astype(BF)
        grad_buf[:, (2 * q + 1) * unit : (2 * q + 2) * unit] = (dh * gate * sig).astype(BF)
    for copy in up_copies:
        copy.wait()
    for c in range(4):
        total = dot_t(grad_buf[...], up_buf[c * piece : (c + 1) * piece, :])
        if not first:
            total = total + base_ref[c]
        if not last:
            out_ref[c] = total
            continue
        for j in range(piece // 128):
            spread[j, pl.ds(c, rows, stride=4), :] = total[:, j * 128 : (j + 1) * 128]
    if last:
        for j in range(piece // 128):
            out_ref[:, j * 128 : (j + 1) * 128] = spread[j].astype(BF)


def back(s, gates, uppers, downs, ups, base, last):
    rows, width = s.shape
    count = len(gates)
    first = base is None
    unit = gates[0].shape[1]
    piece = width // 4
    arrays = []

    def place(array):
        for i, known in enumerate(arrays):
            if known is array:
                return i
        arrays.append(array)
        return len(arrays) - 1

    down_at = [(place(array), index) for array, index in downs]
    up_at = [(place(array), index) for array, index in ups]
    head = [s, *gates, *uppers] + ([] if first else [base])

    def kernel(*refs):
        front, anywhere, tail = refs[: len(head)], refs[len(head) : len(head) + len(arrays)], refs[len(head) + len(arrays) :]
        pick = [(anywhere[i], index) for i, index in down_at + up_at]
        back_kernel(count, first, last, *front, *pick, *tail)

    scratch = [
        pltpu.VMEM((count, unit, width), BF),
        pltpu.VMEM((width, 2 * count * unit), BF),
        pltpu.VMEM((rows, 2 * count * unit), BF),
    ]
    if last:
        scratch.append(pltpu.VMEM((piece // 128, rows * 4, 128), F32))
        out_shape = jax.ShapeDtypeStruct((rows * 4, piece), BF)
    else:
        out_shape = jax.ShapeDtypeStruct((4, rows, piece), F32)
    return pl.pallas_call(
        kernel,
        in_specs=[pl.BlockSpec(memory_space=pltpu.VMEM)] * len(head)
        + [pl.BlockSpec(memory_space=pl.ANY)] * len(arrays),
        out_specs=pl.BlockSpec(memory_space=pltpu.VMEM),
        out_shape=out_shape,
        scratch_shapes=scratch + [pltpu.SemaphoreType.DMA((4 * count,))],
        compiler_params=pltpu.CompilerParams(vmem_limit_bytes=56 << 20),
        name="back_last" if last else "back_first",
        cost_estimate=pl.CostEstimate(
            flops=rows * unit * width, bytes_accessed=6 * unit * width, transcendentals=0
        ),
    )(*head, *arrays)


def parts_of(items, steps, flops, name):
    shapes, in_specs, out_specs = [], [], []
    for array, index in items:
        rows, columns = array[index].shape
        step = rows // steps
        if isinstance(index, int):
            in_specs.append(pl.BlockSpec((None, step, columns), lambda i, index=index: (index, i, 0)))
        else:
            first = index.start // step
            in_specs.append(pl.BlockSpec((step, columns), lambda i, first=first: (first + i, 0)))
        out_specs.append(pl.BlockSpec((step, columns), lambda i: (i, 0)))
        shapes.append(jax.ShapeDtypeStruct((rows, columns), BF))

    def kernel(*refs):
        for i in range(len(items)):
            refs[len(items) + i][...] = refs[i][...]

    return pl.pallas_call(
        kernel,
        grid=(steps,),
        in_specs=in_specs,
        out_specs=out_specs,
        out_shape=shapes,
        name=name,
        cost_estimate=pl.CostEstimate(flops=flops, bytes_accessed=8 << 20, transcendentals=0),
    )(*[array for array, _ in items])


def body(inputs, out_grad, expert_ids, route_weight, gate_up_weight, down_weight, down_moment, down_second):
    experts = lax.axis_size("ep")
    ring = lax.axis_size("edp")
    assert ring == 4
    tok, width = inputs.shape
    top = expert_ids.shape[1]
    capacity = max(2, 3 * tok * top // (2 * experts))
    rows = experts * capacity
    cut = cut_of(width)
    piece = width // cut
    up_ring = [(i, (i + 1) % ring) for i in range(ring)]
    down_ring = [(i, (i - 1) % ring) for i in range(ring)]

    def fwd(x):
        return lax.ppermute(x, "edp", up_ring)

    def bwd(x):
        return lax.ppermute(x, "edp", down_ring)

    def a2a(x):
        shaped = x.reshape(experts, capacity * cut, piece)
        return lax.all_to_all(shaped, "ep", split_axis=0, concat_axis=0, tiled=True)

    dest = pl.pallas_call(
        lambda i, o: slots_kernel(capacity, i, o),
        out_shape=jax.ShapeDtypeStruct((top, tok), jnp.int32),
        name="slots",
    )(expert_ids.T)
    weight = route_weight.T
    block = rows * cut // 4
    sent_rows = make_dispatch(False, cut, rows * cut, width, block)(dest, weight, inputs)
    gate_up, down = gate_up_weight[0], down_weight[0]
    half = down.shape[0] // 2
    left, right = fwd(gate_up), bwd(gate_up)
    recv_rows = a2a(sent_rows)
    la, rb = parts_of([(left, 0), (right, 1)], 7, 4 * 10**9, "parts_up")
    out_grad, left, right, la, rb, down = lax.optimization_barrier((out_grad, left, right, la, rb, down))
    sent_grad = make_dispatch(True, cut, rows * cut, width, block)(dest, weight, out_grad)
    recv_grad = a2a(sent_grad)
    oa, ob = fwd(la), bwd(rb)
    down, oa, ob = lax.optimization_barrier((down, oa, ob))
    down_l, down_r = fwd(down), bwd(down)
    dla, drb = parts_of([(down_l, slice(0, half)), (down_r, slice(half, 2 * half))], 4, 40 * 10**9, "parts_down")
    do0, do1 = fwd(dla), bwd(drb)

    x = recv_rows.reshape(rows, width)
    s = recv_grad.reshape(rows, width)
    ups = [((gate_up, 0), (gate_up, 1)), ((left, 0), (left, 1)), ((right, 0), (right, 1)), ((oa, None), (ob, None))]
    downs = [((down, 0), (down, 1)), ((down_l, 0), (down_l, 1)), ((down_r, 0), (down_r, 1)), ((do0, None), (do1, None))]
    gates, uppers, grads = [], [], []
    for (wg, i), (wu, j) in ups:
        gate = jnp.dot(x, wg if i is None else wg[i], preferred_element_type=F32)
        upper = jnp.dot(x, wu if j is None else wu[j], preferred_element_type=F32)
        gates.append(gate)
        uppers.append(upper)

    def flat(pairs):
        return [piece for pair in pairs for piece in pair]

    partial = back(s, gates[:3], uppers[:3], flat(downs[:3]), flat(ups[:3]), None, False)
    dx = back(s, gates[3:], uppers[3:], [(do0, None), (do1, None)], flat(ups[3:]), partial, True)
    s, dx = lax.optimization_barrier((s, dx))
    grads = []
    for gate, upper in zip(gates, uppers):
        hidden = (gate * jax.nn.sigmoid(gate) * upper).astype(BF)
        grads.append(t_dot(hidden, s))
    returned = a2a(dx).reshape(rows * cut, piece)
    input_grad = combine(dest, returned, width)

    own, left, right, opp = grads
    via_r = fwd(opp[:half].astype(BF))
    via_l = bwd(opp[half:].astype(BF))
    r1 = fwd(right[half:].astype(BF))
    l0 = bwd(left[:half].astype(BF))
    r0 = fwd((right[:half] + via_r.astype(F32)).astype(BF))
    l1 = bwd((left[half:] + via_l.astype(F32)).astype(BF))
    grad0 = own[:half] + r0.astype(F32) + l0.astype(F32)
    grad1 = own[half:] + r1.astype(F32) + l1.astype(F32)
    grad = jnp.concatenate([grad0, grad1], axis=0)
    new_down = adamw(down_weight[0], down_moment[0], down_second[0], grad)[None]
    return (input_grad, new_down)


def solution(mesh):
    placed = (
        P(("ep", "edp"), None),
        P(("ep", "edp"), None),
        P(("ep", "edp"), None),
        P(("ep", "edp"), None),
        P("ep", None, None, "edp"),
        P("ep", "edp", None),
        P("ep", "edp", None),
        P("ep", "edp", None),
    )
    return jax.shard_map(
        body,
        mesh=mesh,
        in_specs=placed,
        out_specs=(P(("ep", "edp"), None), P("ep", "edp", None)),
        check_vma=False,
    )
```

```python
import jax
import jax.numpy as jnp
from jax import lax
from jax.experimental import pallas as pl
from jax.experimental.pallas import tpu as pltpu
from jax.sharding import PartitionSpec as P

BF = jnp.bfloat16
F32 = jnp.float32


def cut_of(width):
    return 4 if width % 512 == 0 else 1


def as_column(row):
    n = row.shape[1]
    eye = lax.broadcasted_iota(jnp.int32, (n, n), 0) == lax.broadcasted_iota(jnp.int32, (n, n), 1)
    return jnp.sum(jnp.where(eye, jnp.broadcast_to(row, (n, n)), 0), axis=1, keepdims=True)


def slots_kernel(capacity, ids_ref, dest_ref):
    top, n = ids_ref.shape
    earlier = lax.broadcasted_iota(jnp.int32, (n, n), 0) < lax.broadcasted_iota(jnp.int32, (n, n), 1)
    columns = [as_column(ids_ref[k : k + 1, :]) for k in range(top)]
    for k in range(top):
        row = ids_ref[k : k + 1, :]
        rank = jnp.zeros((1, n), jnp.int32)
        for j in range(top):
            same = (jnp.broadcast_to(columns[j], (n, n)) == jnp.broadcast_to(row, (n, n))) & earlier
            rank = rank + jnp.sum(same.astype(jnp.int32), axis=0, keepdims=True)
            if j < k:
                rank = rank + (ids_ref[j : j + 1, :] == row).astype(jnp.int32)
        dest_ref[k : k + 1, :] = row * capacity + rank


def make_dispatch(weighted, cut, rows_total, width, block):
    piece = width // cut

    def kernel(dest_ref, weight_ref, rows_ref, out_ref):
        top, n = dest_ref.shape
        base = pl.program_id(0) * block
        index = lax.broadcasted_iota(jnp.int32, (block, cut * n), 0) + base
        part = lax.broadcasted_iota(jnp.int32, (1, cut * n), 1) // n
        hits = []
        for k in range(top):
            key = jnp.concatenate([dest_ref[k : k + 1, :]] * cut, axis=1) * cut + part
            hits.append(index == jnp.broadcast_to(key, index.shape))
        onehot = hits[0]
        for hit in hits[1:]:
            onehot = onehot | hit
        stacked = jnp.concatenate(
            [rows_ref[:, q * piece : (q + 1) * piece] for q in range(cut)], axis=0
        )
        picked = jnp.dot(
            onehot.astype(F32).astype(BF), stacked, preferred_element_type=F32
        )
        if weighted:
            scale = jnp.zeros((block, 1), F32)
            for k in range(top):
                w = jnp.concatenate([weight_ref[k : k + 1, :]] * cut, axis=1)
                scale = scale + jnp.sum(
                    jnp.where(hits[k], jnp.broadcast_to(w, index.shape), 0.0), axis=1, keepdims=True
                )
            picked = picked * scale
        out_ref[...] = picked.astype(BF)

    def call(dest, weight, rows):
        top, n = dest.shape
        return pl.pallas_call(
            kernel,
            grid=(rows_total // block,),
            in_specs=[
                pl.BlockSpec((top, n), lambda i: (0, 0)),
                pl.BlockSpec((top, n), lambda i: (0, 0)),
                pl.BlockSpec((n, width), lambda i: (0, 0)),
            ],
            out_specs=pl.BlockSpec((block, piece), lambda i: (i, 0)),
            out_shape=jax.ShapeDtypeStruct((rows_total, piece), BF),
            compiler_params=pltpu.CompilerParams(vmem_limit_bytes=40 << 20),
            name="dispatch_weighted" if weighted else "dispatch",
            cost_estimate=pl.CostEstimate(
                flops=2 * rows_total * cut * n * piece, bytes_accessed=4 * rows_total * piece, transcendentals=0
            ),
        )(dest, weight, rows)

    return call


def combine(dest, back, width):
    rows_total, piece = back.shape
    cut = width // piece
    top, n = dest.shape

    def kernel(dest_ref, back_ref, out_ref):
        columns = [as_column(dest_ref[k : k + 1, :]) for k in range(top)]
        lane = lax.broadcasted_iota(jnp.int32, (n, rows_total), 1)
        for q in range(cut):
            hit = lane == jnp.broadcast_to(columns[0] * cut + q, lane.shape)
            for k in range(1, top):
                hit = hit | (lane == jnp.broadcast_to(columns[k] * cut + q, lane.shape))
            out_ref[:, q * piece : (q + 1) * piece] = jnp.dot(
                hit.astype(F32).astype(BF), back_ref[...], preferred_element_type=F32
            ).astype(BF)

    return pl.pallas_call(
        kernel,
        out_shape=jax.ShapeDtypeStruct((n, width), BF),
        compiler_params=pltpu.CompilerParams(vmem_limit_bytes=40 << 20),
        name="combine",
        cost_estimate=pl.CostEstimate(
            flops=2 * n * rows_total * width, bytes_accessed=2 * rows_total * piece, transcendentals=0
        ),
    )(dest, back)


def gate_pair(x, up_gate, up_up, flops):
    rows, unit = x.shape[0], up_gate.shape[1]

    def kernel(x_ref, gate_weight, up_weight, gate_ref, upper_ref):
        gate_ref[...] = jnp.dot(x_ref[...], gate_weight[...], preferred_element_type=F32)
        upper_ref[...] = jnp.dot(x_ref[...], up_weight[...], preferred_element_type=F32)

    return pl.pallas_call(
        kernel,
        out_shape=[jax.ShapeDtypeStruct((rows, unit), F32)] * 2,
        compiler_params=pltpu.CompilerParams(vmem_limit_bytes=32 << 20),
        name="gate_pair",
        cost_estimate=pl.CostEstimate(flops=flops, bytes_accessed=12 << 20, transcendentals=0),
    )(x, up_gate, up_up)


def adamw(param, moment, second, own, from_left, from_right, flops):
    rows, width = param.shape
    steps, half = 4, 2
    block = rows // steps

    def kernel(p_ref, m_ref, v_ref, o0_ref, o1_ref, l0_ref, l1_ref, r0_ref, r1_ref, out_ref):
        upper_half = pl.program_id(0) < half
        mine = jnp.where(upper_half, o0_ref[...].astype(F32), o1_ref[...].astype(F32))
        left = jnp.where(upper_half, l0_ref[...].astype(F32), l1_ref[...].astype(F32))
        right = jnp.where(upper_half, r0_ref[...].astype(F32), r1_ref[...].astype(F32))
        grad = mine + right + left
        first = 0.9 * m_ref[...].astype(F32) + 0.1 * grad
        other = 0.95 * v_ref[...].astype(F32) + 0.05 * grad * grad
        first_hat = first / (1.0 - 0.9**10)
        other_hat = other / (1.0 - 0.95**10)
        weight = p_ref[...].astype(F32)
        out_ref[...] = (
            weight - 0.01 * (first_hat / (jnp.sqrt(other_hat) + 1e-08) + 0.1 * weight)
        ).astype(BF)

    whole = pl.BlockSpec((block, width), lambda i: (i, 0))
    low = pl.BlockSpec((block, width), lambda i: (jnp.minimum(i, half - 1), 0))
    high = pl.BlockSpec((block, width), lambda i: (jnp.maximum(i - half, 0), 0))
    return pl.pallas_call(
        kernel,
        grid=(steps,),
        in_specs=[whole] * 3 + [low, high] * 3,
        out_specs=whole,
        out_shape=jax.ShapeDtypeStruct((rows, width), BF),
        compiler_params=pltpu.CompilerParams(vmem_limit_bytes=40 << 20),
        name="adamw",
        cost_estimate=pl.CostEstimate(
            flops=flops, bytes_accessed=16 * rows * width, transcendentals=0
        ),
    )(param, moment, second, *own, *from_left, *from_right)


def dot_t(left, right):
    return lax.dot_general(left, right, (((1,), (1,)), ((), ())), preferred_element_type=F32)


def t_dot(left, right):
    return lax.dot_general(left, right, (((0,), (0,)), ((), ())), preferred_element_type=F32)


def tie(value, *others):
    return lax.optimization_barrier((value,) + others)[0]


def down_copies_of(downs, down_buf, sems, offset):
    half = down_buf.shape[1] // 2
    return [
        pltpu.make_async_copy(
            ref if index is None else ref.at[pl.ds(index * half, half), :],
            down_buf.at[i // 2, pl.ds((i % 2) * half, half), :],
            sems.at[offset + i],
        )
        for i, (ref, index) in enumerate(downs)
    ]


def up_copies_of(ups, up_buf, unit, sems, offset):
    return [
        pltpu.make_async_copy(
            ref if index is None else ref.at[index], up_buf.at[:, pl.ds(i * unit, unit)], sems.at[offset + i]
        )
        for i, (ref, index) in enumerate(ups)
    ]


def write_derivs(q, s_ref, down_buf, gate_ref, upper_ref, grad_buf):
    unit = gate_ref.shape[1]
    dh = dot_t(s_ref[...], down_buf[q])
    gate, upper = gate_ref[...], upper_ref[...]
    sig = jax.nn.sigmoid(gate)
    grad_buf[:, (2 * q) * unit : (2 * q + 1) * unit] = (
        dh * upper * sig * (1.0 + gate * (1.0 - sig))
    ).astype(BF)
    grad_buf[:, (2 * q + 1) * unit : (2 * q + 2) * unit] = (dh * gate * sig).astype(BF)


def first_kernel(count, s_ref, gates, uppers, downs, ups, out_ref, grad_refs, scratch):
    down_buf, up_buf, grad_buf, total_buf, weight_buf, sems = scratch
    unit = gates[0].shape[1]
    half = unit // 2
    piece = total_buf.shape[2]
    down_copies = down_copies_of(downs, down_buf, sems, 0)
    up_copies = up_copies_of(ups, up_buf, unit, sems, 2 * count)
    for copy in down_copies + up_copies:
        copy.start()
    outgoing = []
    for q in (3, 2, 1, 0):
        gate = gates[q][...]
        hidden = jnp.transpose(gate * jax.nn.sigmoid(gate) * uppers[q][...]).astype(BF)
        for c in range(4):
            columns = slice(c * piece, (c + 1) * piece)
            weight_buf[q, :, columns] = jnp.dot(
                hidden, s_ref[:, columns], preferred_element_type=F32
            ).astype(BF)
        for k in range(2):
            copy = pltpu.make_async_copy(
                weight_buf.at[q, pl.ds(k * half, half), :],
                grad_refs[2 * q + k],
                sems.at[4 * count + 2 * q + k],
            )
            copy.start()
            outgoing.append(copy)
    for q in range(count):
        down_copies[2 * q].wait()
        down_copies[2 * q + 1].wait()
        write_derivs(q, s_ref, down_buf, gates[q], uppers[q], grad_buf)
    for copy in up_copies:
        copy.wait()
    for c in range(4):
        total_buf[c] = dot_t(grad_buf[...], up_buf[c * piece : (c + 1) * piece, :])
        copy = pltpu.make_async_copy(total_buf.at[c], out_ref.at[c], sems.at[4 * count + 8 + c])
        copy.start()
        outgoing.append(copy)
    for copy in outgoing:
        copy.wait()


def last_kernel(s_ref, gates, uppers, downs, ups, base_ref, out_ref, scratch):
    down_buf, up_buf, grad_buf, spread, base_buf, sems = scratch
    rows = s_ref.shape[0]
    unit = gates[0].shape[1]
    piece = base_buf.shape[2]
    down_copies = down_copies_of(downs, down_buf, sems, 0)
    up_copies = up_copies_of(ups, up_buf, unit, sems, 2)
    base_copies = [
        pltpu.make_async_copy(base_ref.at[c], base_buf.at[c], sems.at[4 + c]) for c in range(4)
    ]
    for copy in down_copies + up_copies + base_copies:
        copy.start()
    for copy in down_copies:
        copy.wait()
    write_derivs(0, s_ref, down_buf, gates[0], uppers[0], grad_buf)
    for copy in up_copies:
        copy.wait()
    for c in range(4):
        total = dot_t(grad_buf[...], up_buf[c * piece : (c + 1) * piece, :])
        base_copies[c].wait()
        total = total + base_buf[c]
        for j in range(piece // 128):
            spread[j, pl.ds(c, rows, stride=4), :] = total[:, j * 128 : (j + 1) * 128]
    for j in range(piece // 128):
        out_ref[:, j * 128 : (j + 1) * 128] = spread[j].astype(BF)


def back(s, gates, uppers, downs, ups, base):
    rows, width = s.shape
    first = base is None
    count = len(downs) // 2
    unit = gates[0].shape[1]
    piece = width // 4
    arrays = []

    def place(array):
        for i, known in enumerate(arrays):
            if known is array:
                return i
        arrays.append(array)
        return len(arrays) - 1

    down_at = [(place(array), index) for array, index in downs]
    up_at = [(place(array), index) for array, index in ups]
    if not first:
        arrays.append(base)
    held = 1 + len(gates) + len(uppers)

    def kernel(*refs):
        s_ref, g, u = refs[0], refs[1 : 1 + len(gates)], refs[1 + len(gates) : held]
        far, tail = refs[held : held + len(arrays)], refs[held + len(arrays) :]
        down_refs = [(far[i], index) for i, index in down_at]
        up_refs = [(far[i], index) for i, index in up_at]
        if first:
            first_kernel(count, s_ref, g, u, down_refs, up_refs, tail[0], tail[1:9], tail[9:])
        else:
            last_kernel(s_ref, g, u, down_refs, up_refs, far[-1], tail[0], tail[1:])

    vmem = pl.BlockSpec(memory_space=pltpu.VMEM)
    anywhere = pl.BlockSpec(memory_space=pl.ANY)
    scratch = [
        pltpu.VMEM((count, unit, width), BF),
        pltpu.VMEM((width, 2 * count * unit), BF),
        pltpu.VMEM((rows, 2 * count * unit), BF),
    ]
    if first:
        out_shape = [jax.ShapeDtypeStruct((4, rows, piece), F32)]
        out_shape += [jax.ShapeDtypeStruct((unit // 2, width), BF)] * 8
        out_specs = [anywhere] * 9
        scratch += [pltpu.VMEM((4, rows, piece), F32), pltpu.VMEM((4, unit, width), BF)]
        scratch += [pltpu.SemaphoreType.DMA((4 * count + 12,))]
    else:
        out_shape = jax.ShapeDtypeStruct((rows * 4, piece), BF)
        out_specs = vmem
        scratch += [pltpu.VMEM((piece // 128, rows * 4, 128), F32), pltpu.VMEM((4, rows, piece), F32)]
        scratch += [pltpu.SemaphoreType.DMA((8,))]
    return pl.pallas_call(
        kernel,
        in_specs=[vmem] * held + [anywhere] * len(arrays),
        out_specs=out_specs,
        out_shape=out_shape,
        scratch_shapes=scratch,
        compiler_params=pltpu.CompilerParams(vmem_limit_bytes=56 << 20),
        name="back_first" if first else "back_last",
        cost_estimate=pl.CostEstimate(flops=rows * unit * width, bytes_accessed=6 * unit * width, transcendentals=0),
    )(s, *gates, *uppers, *arrays)


def parts_of(items, steps, flops, name):
    shapes, in_specs, out_specs = [], [], []
    for array, index in items:
        rows, columns = array[index].shape
        step = rows // steps
        if isinstance(index, int):
            in_specs.append(pl.BlockSpec((None, step, columns), lambda i, index=index: (index, i, 0)))
        else:
            first = index.start // step
            in_specs.append(pl.BlockSpec((step, columns), lambda i, first=first: (first + i, 0)))
        out_specs.append(pl.BlockSpec((step, columns), lambda i: (i, 0)))
        shapes.append(jax.ShapeDtypeStruct((rows, columns), BF))

    def kernel(*refs):
        for i in range(len(items)):
            refs[len(items) + i][...] = refs[i][...]

    return pl.pallas_call(
        kernel,
        grid=(steps,),
        in_specs=in_specs,
        out_specs=out_specs,
        out_shape=shapes,
        name=name,
        cost_estimate=pl.CostEstimate(flops=flops, bytes_accessed=8 << 20, transcendentals=0),
    )(*[array for array, _ in items])


def body(inputs, out_grad, expert_ids, route_weight, gate_up_weight, down_weight, down_moment, down_second):
    experts = lax.axis_size("ep")
    ring = lax.axis_size("edp")
    assert ring == 4
    tok, width = inputs.shape
    top = expert_ids.shape[1]
    capacity = max(2, 3 * tok * top // (2 * experts))
    rows = experts * capacity
    cut = cut_of(width)
    piece = width // cut
    up_ring = [(i, (i + 1) % ring) for i in range(ring)]
    down_ring = [(i, (i - 1) % ring) for i in range(ring)]

    def fwd(x):
        return lax.ppermute(x, "edp", up_ring)

    def bwd(x):
        return lax.ppermute(x, "edp", down_ring)

    def a2a(x):
        shaped = x.reshape(experts, capacity * cut, piece)
        return lax.all_to_all(shaped, "ep", split_axis=0, concat_axis=0, tiled=True)

    dest = pl.pallas_call(
        lambda i, o: slots_kernel(capacity, i, o),
        out_shape=jax.ShapeDtypeStruct((top, tok), jnp.int32),
        name="slots",
    )(expert_ids.T)
    weight = route_weight.T
    block = rows * cut // 4
    sent_rows = make_dispatch(False, cut, rows * cut, width, block)(dest, weight, inputs)
    gate_up, down = gate_up_weight[0], down_weight[0]
    half = down.shape[0] // 2
    left, right = fwd(gate_up), bwd(gate_up)
    recv_rows = a2a(sent_rows)
    la, rb = parts_of([(left, 0), (right, 1)], 4, 20 * 10**9, "parts_up")
    sent_grad = make_dispatch(True, cut, rows * cut, width, block)(dest, weight, out_grad)
    sent_grad, left, right, la, rb, down = lax.optimization_barrier((sent_grad, left, right, la, rb, down))
    recv_grad = a2a(sent_grad)
    oa, ob = fwd(la), bwd(rb)
    d0, d1, right, oa, ob = lax.optimization_barrier((down[:half], down[half:], right, oa, ob))
    dl0, dr1, dl1, dr0 = fwd(d0), bwd(d1), fwd(d1), bwd(d0)

    x = recv_rows.reshape(rows, width)
    s = recv_grad.reshape(rows, width)
    ups = [((gate_up, 0), (gate_up, 1)), ((left, 0), (left, 1)), ((right, 0), (right, 1)), ((oa, None), (ob, None))]
    gates, uppers = [], []
    for (wg, i), (wu, j) in ups[:3]:
        gates.append(jnp.dot(x, wg[i], preferred_element_type=F32))
        uppers.append(jnp.dot(x, wu[j], preferred_element_type=F32))
    pair = gate_pair(x, oa, ob, 80 * 10**9)
    gates.append(pair[0])
    uppers.append(pair[1])
    dl0, dr1, *held = lax.optimization_barrier((dl0, dr1, *gates, *uppers))
    gates, uppers = held[:4], held[4:]
    do0, do1 = fwd(dl0), bwd(dr1)
    downs = [((down, 0), (down, 1)), ((dl0, None), (dl1, None)), ((dr0, None), (dr1, None)), ((do0, None), (do1, None))]

    def flat(pairs):
        return [piece for pair in pairs for piece in pair]

    partial, *grads = back(s, gates, uppers, flat(downs[:3]), flat(ups[:3]), None)
    partial, do0, do1, *grads = lax.optimization_barrier((partial, do0, do1, *grads))
    dx = back(s, gates[3:], uppers[3:], [(do0, None), (do1, None)], flat(ups[3:]), partial)

    own0, own1, left0, left1, right0, right1, opp0, opp1 = grads
    via_r, via_l = fwd(opp0), bwd(opp1)
    r1, l0 = fwd(right1), bwd(left0)
    via_r, via_l, _ = lax.optimization_barrier((via_r, via_l, dx))
    r0 = fwd((right0.astype(F32) + via_r.astype(F32)).astype(BF))
    l1 = bwd((left1.astype(F32) + via_l.astype(F32)).astype(BF))
    returned = a2a(dx).reshape(rows * cut, piece)
    input_grad = combine(dest, returned, width)
    new_down = adamw(down_weight[0], down_moment[0], down_second[0], (own0, own1), (l0, l1), (r0, r1), 20 * 10**9)[None]
    return (input_grad, new_down)


def solution(mesh):
    placed = (
        P(("ep", "edp"), None),
        P(("ep", "edp"), None),
        P(("ep", "edp"), None),
        P(("ep", "edp"), None),
        P("ep", None, None, "edp"),
        P("ep", "edp", None),
        P("ep", "edp", None),
        P("ep", "edp", None),
    )
    return jax.shard_map(
        body,
        mesh=mesh,
        in_specs=placed,
        out_specs=(P(("ep", "edp"), None), P("ep", "edp", None)),
        check_vma=False,
    )
```

```python
import jax
import jax.numpy as jnp
from jax import lax
from jax.experimental import pallas as pl
from jax.experimental.pallas import tpu as pltpu
from jax.sharding import PartitionSpec as P

BF = jnp.bfloat16
F32 = jnp.float32


def cut_of(width):
    return 4 if width % 512 == 0 else 1


def as_column(row):
    n = row.shape[1]
    eye = lax.broadcasted_iota(jnp.int32, (n, n), 0) == lax.broadcasted_iota(jnp.int32, (n, n), 1)
    return jnp.sum(jnp.where(eye, jnp.broadcast_to(row, (n, n)), 0), axis=1, keepdims=True)


def slots_kernel(capacity, ids_ref, dest_ref):
    top, n = ids_ref.shape
    earlier = lax.broadcasted_iota(jnp.int32, (n, n), 0) < lax.broadcasted_iota(jnp.int32, (n, n), 1)
    columns = [as_column(ids_ref[k : k + 1, :]) for k in range(top)]
    for k in range(top):
        row = ids_ref[k : k + 1, :]
        rank = jnp.zeros((1, n), jnp.int32)
        for j in range(top):
            same = (jnp.broadcast_to(columns[j], (n, n)) == jnp.broadcast_to(row, (n, n))) & earlier
            rank = rank + jnp.sum(same.astype(jnp.int32), axis=0, keepdims=True)
            if j < k:
                rank = rank + (ids_ref[j : j + 1, :] == row).astype(jnp.int32)
        dest_ref[k : k + 1, :] = row * capacity + rank


def make_dispatch(weighted, cut, rows_total, width, block):
    piece = width // cut

    def kernel(dest_ref, weight_ref, rows_ref, out_ref):
        top, n = dest_ref.shape
        base = pl.program_id(0) * block
        index = lax.broadcasted_iota(jnp.int32, (block, cut * n), 0) + base
        part = lax.broadcasted_iota(jnp.int32, (1, cut * n), 1) // n
        hits = []
        for k in range(top):
            key = jnp.concatenate([dest_ref[k : k + 1, :]] * cut, axis=1) * cut + part
            hits.append(index == jnp.broadcast_to(key, index.shape))
        onehot = hits[0]
        for hit in hits[1:]:
            onehot = onehot | hit
        stacked = jnp.concatenate(
            [rows_ref[:, q * piece : (q + 1) * piece] for q in range(cut)], axis=0
        )
        picked = jnp.dot(
            onehot.astype(F32).astype(BF), stacked, preferred_element_type=F32
        )
        if weighted:
            scale = jnp.zeros((block, 1), F32)
            for k in range(top):
                w = jnp.concatenate([weight_ref[k : k + 1, :]] * cut, axis=1)
                scale = scale + jnp.sum(
                    jnp.where(hits[k], jnp.broadcast_to(w, index.shape), 0.0), axis=1, keepdims=True
                )
            picked = picked * scale
        out_ref[...] = picked.astype(BF)

    def call(dest, weight, rows):
        top, n = dest.shape
        return pl.pallas_call(
            kernel,
            grid=(rows_total // block,),
            in_specs=[
                pl.BlockSpec((top, n), lambda i: (0, 0)),
                pl.BlockSpec((top, n), lambda i: (0, 0)),
                pl.BlockSpec((n, width), lambda i: (0, 0)),
            ],
            out_specs=pl.BlockSpec((block, piece), lambda i: (i, 0)),
            out_shape=jax.ShapeDtypeStruct((rows_total, piece), BF),
            compiler_params=pltpu.CompilerParams(vmem_limit_bytes=40 << 20),
            name="dispatch_weighted" if weighted else "dispatch",
            cost_estimate=pl.CostEstimate(
                flops=2 * rows_total * cut * n * piece, bytes_accessed=4 * rows_total * piece, transcendentals=0
            ),
        )(dest, weight, rows)

    return call


def combine(dest, back, width):
    rows_total, piece = back.shape
    cut = width // piece
    top, n = dest.shape

    def kernel(dest_ref, back_ref, out_ref):
        columns = [as_column(dest_ref[k : k + 1, :]) for k in range(top)]
        lane = lax.broadcasted_iota(jnp.int32, (n, rows_total), 1)
        for q in range(cut):
            hit = lane == jnp.broadcast_to(columns[0] * cut + q, lane.shape)
            for k in range(1, top):
                hit = hit | (lane == jnp.broadcast_to(columns[k] * cut + q, lane.shape))
            out_ref[:, q * piece : (q + 1) * piece] = jnp.dot(
                hit.astype(F32).astype(BF), back_ref[...], preferred_element_type=F32
            ).astype(BF)

    return pl.pallas_call(
        kernel,
        out_shape=jax.ShapeDtypeStruct((n, width), BF),
        compiler_params=pltpu.CompilerParams(vmem_limit_bytes=40 << 20),
        name="combine",
        cost_estimate=pl.CostEstimate(
            flops=2 * n * rows_total * width, bytes_accessed=2 * rows_total * piece, transcendentals=0
        ),
    )(dest, back)


def gate_pair(x, up_gate, up_up, flops):
    rows, unit = x.shape[0], up_gate.shape[1]

    def kernel(x_ref, gate_weight, up_weight, gate_ref, upper_ref):
        gate_ref[...] = jnp.dot(x_ref[...], gate_weight[...], preferred_element_type=F32)
        upper_ref[...] = jnp.dot(x_ref[...], up_weight[...], preferred_element_type=F32)

    return pl.pallas_call(
        kernel,
        out_shape=[jax.ShapeDtypeStruct((rows, unit), F32)] * 2,
        compiler_params=pltpu.CompilerParams(vmem_limit_bytes=32 << 20),
        name="gate_pair",
        cost_estimate=pl.CostEstimate(flops=flops, bytes_accessed=12 << 20, transcendentals=0),
    )(x, up_gate, up_up)


def adamw(param, moment, second, own, from_left, from_right, flops):
    rows, width = param.shape
    steps, half = 4, 2
    block = rows // steps

    def kernel(p_ref, m_ref, v_ref, o0_ref, o1_ref, l0_ref, l1_ref, r0_ref, r1_ref, out_ref):
        upper_half = pl.program_id(0) < half
        mine = jnp.where(upper_half, o0_ref[...].astype(F32), o1_ref[...].astype(F32))
        left = jnp.where(upper_half, l0_ref[...].astype(F32), l1_ref[...].astype(F32))
        right = jnp.where(upper_half, r0_ref[...].astype(F32), r1_ref[...].astype(F32))
        grad = mine + right + left
        first = 0.9 * m_ref[...].astype(F32) + 0.1 * grad
        other = 0.95 * v_ref[...].astype(F32) + 0.05 * grad * grad
        first_hat = first / (1.0 - 0.9**10)
        other_hat = other / (1.0 - 0.95**10)
        weight = p_ref[...].astype(F32)
        out_ref[...] = (
            weight - 0.01 * (first_hat / (jnp.sqrt(other_hat) + 1e-08) + 0.1 * weight)
        ).astype(BF)

    whole = pl.BlockSpec((block, width), lambda i: (i, 0))
    low = pl.BlockSpec((block, width), lambda i: (jnp.minimum(i, half - 1), 0))
    high = pl.BlockSpec((block, width), lambda i: (jnp.maximum(i - half, 0), 0))
    return pl.pallas_call(
        kernel,
        grid=(steps,),
        in_specs=[whole] * 3 + [low, high] * 3,
        out_specs=whole,
        out_shape=jax.ShapeDtypeStruct((rows, width), BF),
        compiler_params=pltpu.CompilerParams(vmem_limit_bytes=40 << 20),
        name="adamw",
        cost_estimate=pl.CostEstimate(
            flops=flops, bytes_accessed=16 * rows * width, transcendentals=0
        ),
    )(param, moment, second, *own, *from_left, *from_right)


def dot_t(left, right):
    return lax.dot_general(left, right, (((1,), (1,)), ((), ())), preferred_element_type=F32)


def t_dot(left, right):
    return lax.dot_general(left, right, (((0,), (0,)), ((), ())), preferred_element_type=F32)


def tie(value, *others):
    return lax.optimization_barrier((value,) + others)[0]


def down_copies_of(downs, down_buf, sems, offset):
    half = down_buf.shape[1] // 2
    return [
        pltpu.make_async_copy(
            ref if index is None else ref.at[pl.ds(index * half, half), :],
            down_buf.at[i // 2, pl.ds((i % 2) * half, half), :],
            sems.at[offset + i],
        )
        for i, (ref, index) in enumerate(downs)
    ]


def up_copies_of(ups, up_buf, unit, sems, offset):
    return [
        pltpu.make_async_copy(
            ref if index is None else ref.at[index], up_buf.at[:, pl.ds(i * unit, unit)], sems.at[offset + i]
        )
        for i, (ref, index) in enumerate(ups)
    ]


def write_derivs(q, s_ref, down_buf, gate_ref, upper_ref, grad_buf):
    unit = gate_ref.shape[1]
    dh = dot_t(s_ref[...], down_buf[q])
    gate, upper = gate_ref[...], upper_ref[...]
    sig = jax.nn.sigmoid(gate)
    grad_buf[:, (2 * q) * unit : (2 * q + 1) * unit] = (
        dh * upper * sig * (1.0 + gate * (1.0 - sig))
    ).astype(BF)
    grad_buf[:, (2 * q + 1) * unit : (2 * q + 2) * unit] = (dh * gate * sig).astype(BF)


def first_kernel(count, s_ref, gates, uppers, downs, ups, out_ref, grad_refs, scratch):
    down_buf, up_buf, grad_buf, total_buf, weight_buf, sems = scratch
    unit = gates[0].shape[1]
    half = unit // 2
    piece = total_buf.shape[2]
    down_copies = down_copies_of(downs, down_buf, sems, 0)
    up_copies = up_copies_of(ups, up_buf, unit, sems, 2 * count)
    for copy in down_copies + up_copies:
        copy.start()
    outgoing = []
    for q in (3, 2, 1, 0):
        gate = gates[q][...]
        hidden = jnp.transpose(gate * jax.nn.sigmoid(gate) * uppers[q][...]).astype(BF)
        for c in range(4):
            columns = slice(c * piece, (c + 1) * piece)
            weight_buf[q, :, columns] = jnp.dot(
                hidden, s_ref[:, columns], preferred_element_type=F32
            ).astype(BF)
        for k in range(2):
            copy = pltpu.make_async_copy(
                weight_buf.at[q, pl.ds(k * half, half), :],
                grad_refs[2 * q + k],
                sems.at[4 * count + 2 * q + k],
            )
            copy.start()
            outgoing.append(copy)
    for q in range(count):
        down_copies[2 * q].wait()
        down_copies[2 * q + 1].wait()
        write_derivs(q, s_ref, down_buf, gates[q], uppers[q], grad_buf)
    for copy in up_copies:
        copy.wait()
    for c in range(4):
        total_buf[c] = dot_t(grad_buf[...], up_buf[c * piece : (c + 1) * piece, :]).astype(BF)
        copy = pltpu.make_async_copy(total_buf.at[c], out_ref.at[c], sems.at[4 * count + 8 + c])
        copy.start()
        outgoing.append(copy)
    for copy in outgoing:
        copy.wait()


def last_kernel(s_ref, gates, uppers, downs, ups, base_ref, out_ref, scratch):
    down_buf, up_buf, grad_buf, spread, base_buf, sems = scratch
    rows = s_ref.shape[0]
    unit = gates[0].shape[1]
    piece = base_buf.shape[2]
    down_copies = down_copies_of(downs, down_buf, sems, 0)
    up_copies = up_copies_of(ups, up_buf, unit, sems, 2)
    base_copies = [
        pltpu.make_async_copy(base_ref.at[c], base_buf.at[c], sems.at[4 + c]) for c in range(4)
    ]
    for copy in down_copies + up_copies + base_copies:
        copy.start()
    for copy in down_copies:
        copy.wait()
    write_derivs(0, s_ref, down_buf, gates[0], uppers[0], grad_buf)
    for copy in up_copies:
        copy.wait()
    for c in range(4):
        total = dot_t(grad_buf[...], up_buf[c * piece : (c + 1) * piece, :])
        base_copies[c].wait()
        total = total + base_buf[c].astype(F32)
        for j in range(piece // 128):
            spread[j, pl.ds(c, rows, stride=4), :] = total[:, j * 128 : (j + 1) * 128]
    for j in range(piece // 128):
        out_ref[:, j * 128 : (j + 1) * 128] = spread[j].astype(BF)


def back(s, gates, uppers, downs, ups, base):
    rows, width = s.shape
    first = base is None
    count = len(downs) // 2
    unit = gates[0].shape[1]
    piece = width // 4
    arrays = []

    def place(array):
        for i, known in enumerate(arrays):
            if known is array:
                return i
        arrays.append(array)
        return len(arrays) - 1

    down_at = [(place(array), index) for array, index in downs]
    up_at = [(place(array), index) for array, index in ups]
    if not first:
        arrays.append(base)
    held = 1 + len(gates) + len(uppers)

    def kernel(*refs):
        s_ref, g, u = refs[0], refs[1 : 1 + len(gates)], refs[1 + len(gates) : held]
        far, tail = refs[held : held + len(arrays)], refs[held + len(arrays) :]
        down_refs = [(far[i], index) for i, index in down_at]
        up_refs = [(far[i], index) for i, index in up_at]
        if first:
            first_kernel(count, s_ref, g, u, down_refs, up_refs, tail[0], tail[1:9], tail[9:])
        else:
            last_kernel(s_ref, g, u, down_refs, up_refs, far[-1], tail[0], tail[1:])

    vmem = pl.BlockSpec(memory_space=pltpu.VMEM)
    anywhere = pl.BlockSpec(memory_space=pl.ANY)
    scratch = [
        pltpu.VMEM((count, unit, width), BF),
        pltpu.VMEM((width, 2 * count * unit), BF),
        pltpu.VMEM((rows, 2 * count * unit), BF),
    ]
    if first:
        out_shape = [jax.ShapeDtypeStruct((4, rows, piece), BF)]
        out_shape += [jax.ShapeDtypeStruct((unit // 2, width), BF)] * 8
        out_specs = [anywhere] * 9
        scratch += [pltpu.VMEM((4, rows, piece), BF), pltpu.VMEM((4, unit, width), BF)]
        scratch += [pltpu.SemaphoreType.DMA((4 * count + 12,))]
    else:
        out_shape = jax.ShapeDtypeStruct((rows * 4, piece), BF)
        out_specs = vmem
        scratch += [pltpu.VMEM((piece // 128, rows * 4, 128), F32), pltpu.VMEM((4, rows, piece), BF)]
        scratch += [pltpu.SemaphoreType.DMA((8,))]
    return pl.pallas_call(
        kernel,
        in_specs=[vmem] * held + [anywhere] * len(arrays),
        out_specs=out_specs,
        out_shape=out_shape,
        scratch_shapes=scratch,
        compiler_params=pltpu.CompilerParams(vmem_limit_bytes=56 << 20),
        name="back_first" if first else "back_last",
        cost_estimate=pl.CostEstimate(flops=rows * unit * width, bytes_accessed=6 * unit * width, transcendentals=0),
    )(s, *gates, *uppers, *arrays)


def parts_of(items, steps, flops, name):
    n = len(items)
    rows, columns = items[0][0].shape[1:]
    step = rows // steps

    def kernel(*refs):
        held, sems_in, sems_out = refs[2 * n :]
        moves = []
        for j in range(steps):
            window = pl.ds(j * step, step)
            for i, (_, index) in enumerate(items):
                moves.append(
                    (
                        pltpu.make_async_copy(
                            refs[i].at[index, window, :], held.at[i, window, :], sems_in.at[n * j + i]
                        ),
                        pltpu.make_async_copy(
                            held.at[i, window, :], refs[n + i].at[window, :], sems_out.at[n * j + i]
                        ),
                    )
                )
        for inward, _ in moves:
            inward.start()
        for inward, outward in moves:
            inward.wait()
            outward.start()
        for _, outward in moves:
            outward.wait()

    anywhere = pl.BlockSpec(memory_space=pl.ANY)
    return pl.pallas_call(
        kernel,
        in_specs=[anywhere] * n,
        out_specs=[anywhere] * n,
        out_shape=[jax.ShapeDtypeStruct((rows, columns), BF)] * n,
        scratch_shapes=[
            pltpu.VMEM((n, rows, columns), BF),
            pltpu.SemaphoreType.DMA((n * steps,)),
            pltpu.SemaphoreType.DMA((n * steps,)),
        ],
        compiler_params=pltpu.CompilerParams(vmem_limit_bytes=8 << 20),
        name=name,
        cost_estimate=pl.CostEstimate(flops=flops, bytes_accessed=8 << 20, transcendentals=0),
    )(*[array for array, _ in items])


def body(inputs, out_grad, expert_ids, route_weight, gate_up_weight, down_weight, down_moment, down_second):
    experts = lax.axis_size("ep")
    ring = lax.axis_size("edp")
    assert ring == 4
    tok, width = inputs.shape
    top = expert_ids.shape[1]
    capacity = max(2, 3 * tok * top // (2 * experts))
    rows = experts * capacity
    cut = cut_of(width)
    piece = width // cut
    up_ring = [(i, (i + 1) % ring) for i in range(ring)]
    down_ring = [(i, (i - 1) % ring) for i in range(ring)]

    def fwd(x):
        return lax.ppermute(x, "edp", up_ring)

    def bwd(x):
        return lax.ppermute(x, "edp", down_ring)

    def a2a(x):
        shaped = x.reshape(experts, capacity * cut, piece)
        return lax.all_to_all(shaped, "ep", split_axis=0, concat_axis=0, tiled=True)

    dest = pl.pallas_call(
        lambda i, o: slots_kernel(capacity, i, o),
        out_shape=jax.ShapeDtypeStruct((top, tok), jnp.int32),
        name="slots",
    )(expert_ids.T)
    weight = route_weight.T
    block = rows * cut // 4
    sent_rows = make_dispatch(False, cut, rows * cut, width, block)(dest, weight, inputs)
    gate_up, down = gate_up_weight[0], down_weight[0]
    half = down.shape[0] // 2
    left, right = fwd(gate_up), bwd(gate_up)
    recv_rows = a2a(sent_rows)
    d0, d1 = down[:half], down[half:]
    left, right, d0, d1 = lax.optimization_barrier((left, right, d0, d1))
    la, rb = parts_of([(left, 0), (right, 1)], 4, 20 * 10**9, "parts_up")
    sent_grad = make_dispatch(True, cut, rows * cut, width, block)(dest, weight, out_grad)
    sent_grad, left, right, la, rb, down = lax.optimization_barrier((sent_grad, left, right, la, rb, down))
    recv_grad = a2a(sent_grad)
    oa, ob = fwd(la), bwd(rb)
    d0, d1, right, oa, ob = lax.optimization_barrier((d0, d1, right, oa, ob))
    dl0, dr1, dl1, dr0 = fwd(d0), bwd(d1), fwd(d1), bwd(d0)

    x = recv_rows.reshape(rows, width)
    s = recv_grad.reshape(rows, width)
    ups = [((gate_up, 0), (gate_up, 1)), ((left, 0), (left, 1)), ((right, 0), (right, 1)), ((oa, None), (ob, None))]
    gates, uppers = [], []
    for (wg, i), (wu, j) in ups[:3]:
        gates.append(jnp.dot(x, wg[i], preferred_element_type=F32))
        uppers.append(jnp.dot(x, wu[j], preferred_element_type=F32))
    pair = gate_pair(x, oa, ob, 80 * 10**9)
    gates.append(pair[0])
    uppers.append(pair[1])
    dl0, dr1, *held = lax.optimization_barrier((dl0, dr1, *gates, *uppers))
    gates, uppers = held[:4], held[4:]
    do0, do1 = fwd(dl0), bwd(dr1)
    downs = [((down, 0), (down, 1)), ((dl0, None), (dl1, None)), ((dr0, None), (dr1, None)), ((do0, None), (do1, None))]

    def flat(pairs):
        return [piece for pair in pairs for piece in pair]

    partial, *grads = back(s, gates, uppers, flat(downs[:3]), flat(ups[:3]), None)
    partial, do0, do1, *grads = lax.optimization_barrier((partial, do0, do1, *grads))
    dx = back(s, gates[3:], uppers[3:], [(do0, None), (do1, None)], flat(ups[3:]), partial)

    own0, own1, left0, left1, right0, right1, opp0, opp1 = grads
    via_r, via_l = fwd(opp0), bwd(opp1)
    r1, l0 = fwd(right1), bwd(left0)
    via_r, via_l, _ = lax.optimization_barrier((via_r, via_l, dx))
    r0 = fwd((right0.astype(F32) + via_r.astype(F32)).astype(BF))
    l1 = bwd((left1.astype(F32) + via_l.astype(F32)).astype(BF))
    returned = a2a(dx).reshape(rows * cut, piece)
    input_grad = combine(dest, returned, width)
    new_down = adamw(down_weight[0], down_moment[0], down_second[0], (own0, own1), (l0, l1), (r0, r1), 20 * 10**9)[None]
    return (input_grad, new_down)


def solution(mesh):
    placed = (
        P(("ep", "edp"), None),
        P(("ep", "edp"), None),
        P(("ep", "edp"), None),
        P(("ep", "edp"), None),
        P("ep", None, None, "edp"),
        P("ep", "edp", None),
        P("ep", "edp", None),
        P("ep", "edp", None),
    )
    return jax.shard_map(
        body,
        mesh=mesh,
        in_specs=placed,
        out_specs=(P(("ep", "edp"), None), P("ep", "edp", None)),
        check_vma=False,
    )
```
